256 devices in a mesh: dp: 32 (over x, y, core), rep: 8 (over z).
Axes of the slice: x: 4, y: 4, z: 8, core: 2. Of those that a mesh axis runs over, the one named last changes fastest.
Arguments:
- residual_in: bfloat16 [2048, 3584], P(('rep', 'dp')), parts along dimension 0, may hold values from -3 to 3
- q_latent: bfloat16 [2048, 128, 512], P(('rep', 'dp')), parts along dimension 0
- q_rope: bfloat16 [2048, 64, 128], P(('rep', 'dp')), parts along dimension 0, may hold values from -6 to 6
- cache_latent: bfloat16 [2048, 384, 512], P(('rep', 'dp')), parts along dimension 0
- cache_rope: bfloat16 [2048, 64, 384], P(('rep', 'dp')), parts along dimension 0, may hold values from -6 to 6
- new_latent: bfloat16 [2048, 512], P(('rep', 'dp')), parts along dimension 0, may hold values from -6 to 6
- new_rope: bfloat16 [2048, 64], P(('rep', 'dp')), parts along dimension 0, may hold values from -6 to 6
- lengths: int32 [2048], P(('rep', 'dp')), parts along dimension 0, may hold values from 1 to 384, as said below
- counts: int32 [256], P(('rep', 'dp')), parts along dimension 0, may hold values from 1 to 8, as said below
- w_uv: bfloat16 [128, 512, 128], P('dp'), may hold values from -0.5 to 0.5
- w_o: bfloat16 [16384, 3584], P('dp'), may hold values from -0.125 to 0.125
- norm_gain: bfloat16 [3584], replicated, may hold values from 0.099609375 to 1.8984375
- w_gate: bfloat16 [3584, 9216], P(None, 'dp'), may hold values from -0.09375 to 0.09375
- w_up: bfloat16 [3584, 9216], P(None, 'dp'), may hold values from -0.09375 to 0.09375
- w_down: bfloat16 [9216, 3584], P('dp'), may hold values from -0.125 to 0.125
Outputs:
- layer_out: bfloat16 [2048, 3584], P(('rep', 'dp')), parts along dimension 0
The draws below stay inside these ranges and needn't reach their ends.
There are 8 independent parts, one for each index of `rep`. The reference program is written for one: setup_inputs(seed, part) draws one part's arguments, and reference() takes and returns one part's arrays. A program takes and returns all parts, laid end to end along the dimension named above; an argument that names none is the same for every part. Nothing has to cross between parts.
Inputs may be any that keep to these rules, and one draw needn't show every extreme that they name: `lengths`: every value at least 1; some live slot of a heavily loaded device holds exactly 384 positions. `counts`: some device has all 8 slots live.
All inputs are finite; a program needn't handle non-finite values.
Results may differ from the reference program's by a relative error of at most 0.024.
Values may be sent and summed in bfloat16 or wider, within the bound.
No kernel may reach another device: no remote copies, remote signals or barrier semaphores. Data moves between devices by JAX's collectives and lax.ppermute only.
A program may use at most 64 MiB of HBM per device.

```python
import jax
import jax.numpy as jnp
from jax import lax

D = 3584
FF = 9216
H = 128
LAT = 512
ROPE = 64
HV = 128
R_DEV = 8
L_MAX = 384
B_ALL = 256
N_DP = 32


def draw_cache_latent(key, part):
    key = jax.random.fold_in(key, 11)
    first_key = jax.random.fold_in(key, 0)
    base = jax.random.normal(first_key, (B_ALL, L_MAX, LAT), jnp.float32)
    return jnp.clip(base, -6.0, 6.0).astype(jnp.bfloat16)


def draw_q_latent(key, part):
    key = jax.random.fold_in(key, 12)
    base = jax.random.normal(key, (B_ALL, H, LAT), jnp.float32)
    return base.astype(jnp.bfloat16)


def draw_counts(key, part):
    key = jax.random.fold_in(key, 13)
    first_key, second_key = jax.random.split(key)
    values = jax.random.randint(first_key, (N_DP,), 1, R_DEV + 1)
    chosen = jax.random.randint(second_key, (), 0, N_DP)
    return values.at[chosen].set(R_DEV).astype(jnp.int32)


def draw_lengths(key, part):
    key = jax.random.fold_in(key, 14)
    first_key, second_key, third_key = jax.random.split(key, 3)
    heavy = jax.random.randint(first_key, (N_DP,), 0, 4) == 0
    chosen = jax.random.randint(second_key, (), 0, N_DP)
    heavy = heavy.at[chosen].set(True)
    limit = jnp.where(heavy, L_MAX, L_MAX // 4)
    limit = jnp.repeat(limit, R_DEV)
    fraction = jax.random.randint(third_key, (B_ALL,), 0, 1 << 20)
    values = 1 + fraction * limit // (1 << 20)
    values = values.at[chosen * R_DEV].set(L_MAX)
    return values.astype(jnp.int32)


def block_levels(key, shape, cuts, low, top_value):
    def one(dim, shards_of):
        draws = jax.random.uniform(jax.random.fold_in(jax.random.fold_in(key, 6), dim), (shards_of,), jnp.float32, low / len(cuts), top_value / len(cuts))
        return jnp.repeat(jnp.exp(draws), shape[dim] // shards_of).reshape((-1,) + (1,) * (len(shape) - dim - 1))

    gain = one(*cuts[0])
    for cut in cuts[1:]:
        gain = gain * one(*cut)
    return gain


def bell_draw(stream_key, dims, scale, reach, pieces=(), held_as=jnp.bfloat16):
    values = scale * jax.random.normal(stream_key, dims, jnp.float32)
    if pieces:
        values = values * block_levels(stream_key, dims, pieces, -0.22, 0.18)
    return jnp.clip(values, -reach, reach).astype(held_as)


def setup_inputs(seed: int = 0, part: int = 0) -> dict:
    keys = jax.random.split(jax.random.key(seed), 16)
    part_splits = jax.random.split(jax.random.fold_in(keys[15], part), 16)
    residual_in = bell_draw(part_splits[0], (B_ALL, D), 0.5, 3.0, ((0, 32),))
    q_latent = draw_q_latent(jax.random.fold_in(jax.random.fold_in(keys[15], part), 71), part)
    q_rope = bell_draw(part_splits[2], (B_ALL, ROPE, H), 1.0, 6.0, ((0, 32),))
    cache_latent = draw_cache_latent(jax.random.fold_in(jax.random.fold_in(keys[15], part), 71), part)
    cache_rope = bell_draw(part_splits[4], (B_ALL, ROPE, L_MAX), 1.0, 6.0, ((0, 32),))
    new_latent = bell_draw(part_splits[5], (B_ALL, LAT), 1.0, 6.0, ((0, 32),))
    new_rope = bell_draw(part_splits[6], (B_ALL, ROPE), 1.0, 6.0, ((0, 32),))
    lengths = draw_lengths(jax.random.fold_in(jax.random.fold_in(keys[15], part), 71), part)
    counts = draw_counts(jax.random.fold_in(jax.random.fold_in(keys[15], part), 71), part)
    w_uv = bell_draw(keys[9], (H, LAT, HV), HV ** -0.5, 0.5, ((0, 32),))
    w_o = bell_draw(keys[10], (H * HV, D), (H * 16) ** -0.5, 0.125, ((0, 32),))
    norm_gain = jnp.clip(1.0 + 0.18 * jax.random.normal(keys[11], (D,), jnp.float32), 0.099609375, 1.8984375).astype(jnp.bfloat16)
    w_gate = bell_draw(keys[12], (D, FF), D ** -0.5, 0.09375, ((1, 32),))
    w_up = bell_draw(keys[13], (D, FF), D ** -0.5, 0.09375, ((1, 32),))
    w_down = bell_draw(keys[14], (FF, D), (FF // 4) ** -0.5, 0.125, ((0, 32),))
    return dict(residual_in=residual_in, q_latent=q_latent, q_rope=q_rope, cache_latent=cache_latent, cache_rope=cache_rope, new_latent=new_latent, new_rope=new_rope, lengths=lengths, counts=counts, w_uv=w_uv, w_o=w_o, norm_gain=norm_gain, w_gate=w_gate, w_up=w_up, w_down=w_down)


def attend_one(items):
    q_lat, q_rot, cache_lat, cache_rot, fresh_lat, fresh_rot, used_len = items
    score_scale = (HV + ROPE) ** (-0.5)
    scores = jnp.einsum('hj,pj->hp', q_lat.astype(jnp.float32), cache_lat.astype(jnp.float32))
    scores = scores + jnp.einsum('rh,rp->hp', q_rot.astype(jnp.float32), cache_rot.astype(jnp.float32))
    scores = scores * score_scale
    fresh_score = (jnp.einsum('hj,j->h', q_lat.astype(jnp.float32), fresh_lat.astype(jnp.float32)) + jnp.einsum('rh,r->h', q_rot.astype(jnp.float32), fresh_rot.astype(jnp.float32))) * score_scale
    key_mask = jnp.arange(L_MAX, dtype=jnp.int32) < used_len
    scores = jnp.where(key_mask[None, :], scores, -jnp.inf)
    top = jnp.maximum(lax.optimization_barrier(jnp.max(scores, axis=1)), fresh_score)
    expo = jnp.exp(scores - top[:, None])
    fresh_expo = jnp.exp(fresh_score - top)
    total = lax.optimization_barrier(jnp.sum(expo, axis=1)) + fresh_expo
    probs = (expo / total[:, None]).astype(jnp.bfloat16)
    fresh_prob = (fresh_expo / total).astype(jnp.bfloat16)
    out = jnp.einsum('hp,pj->hj', probs.astype(jnp.float32), cache_lat.astype(jnp.float32))
    out = out + fresh_prob.astype(jnp.float32)[:, None] * fresh_lat.astype(jnp.float32)[None, :]
    return out.astype(jnp.bfloat16)

def reference(residual_in, q_latent, q_rope, cache_latent, cache_rope, new_latent, new_rope, lengths, counts, w_uv, w_o, norm_gain, w_gate, w_up, w_down):
    slot_ids = jnp.arange(B_ALL, dtype=jnp.int32)
    live_slot = slot_ids % R_DEV < counts[slot_ids // R_DEV]
    used = jnp.where(live_slot, lengths, 0).astype(jnp.int32)
    o_latent = lax.map(attend_one, (q_latent, q_rope, cache_latent, cache_rope, new_latent, new_rope, used))
    heads_v = jnp.einsum('bhj,hjk->bhk', o_latent.astype(jnp.float32), w_uv.astype(jnp.float32)).astype(jnp.bfloat16)
    attn = jnp.dot(heads_v.reshape(B_ALL, H * HV), w_o, preferred_element_type=jnp.float32)
    hidden = residual_in.astype(jnp.float32) + attn
    normed = hidden * lax.rsqrt(lax.optimization_barrier(jnp.mean(hidden * hidden, axis=-1, keepdims=True)) + 1e-06)
    normed = (normed * norm_gain.astype(jnp.float32)).astype(jnp.bfloat16)
    gate = jnp.dot(normed, w_gate, preferred_element_type=jnp.float32)
    upper = jnp.dot(normed, w_up, preferred_element_type=jnp.float32)
    activated = (jax.nn.silu(gate) * upper).astype(jnp.bfloat16)
    ffn = jnp.dot(activated, w_down, preferred_element_type=jnp.float32)
    return (hidden + ffn).astype(jnp.bfloat16)
```

```python
import jax
import jax.numpy as jnp
from jax import lax
from jax.sharding import PartitionSpec as P


def normalize(values, gain):
    scaled = values * lax.rsqrt(jnp.mean(values * values, axis=-1, keepdims=True) + 1e-06)
    return (scaled * gain.astype(jnp.float32)).astype(jnp.bfloat16)


def attend(
    q_latent, q_rope, cache_latent, cache_rope, new_latent, new_rope, lengths, counts, score_scale
):
    row_count, positions = cache_latent.shape[:2]
    live_slot = jnp.arange(row_count, dtype=jnp.int32) < counts[0]
    used_len = jnp.where(live_slot, lengths, 0)
    scores = jnp.einsum("bhj,bpj->bhp", q_latent, cache_latent, preferred_element_type=jnp.float32)
    scores = scores + jnp.einsum(
        "brh,brp->bhp", q_rope, cache_rope, preferred_element_type=jnp.float32
    )
    scores = scores * score_scale
    fresh_score = (
        jnp.einsum("bhj,bj->bh", q_latent, new_latent, preferred_element_type=jnp.float32)
        + jnp.einsum("brh,br->bh", q_rope, new_rope, preferred_element_type=jnp.float32)
    ) * score_scale
    key_mask = jnp.arange(positions, dtype=jnp.int32)[None, :] < used_len[:, None]
    scores = jnp.where(key_mask[:, None, :], scores, -jnp.inf)
    top = jnp.maximum(jnp.max(scores, axis=2), fresh_score)
    expo = jnp.exp(scores - top[:, :, None])
    fresh_expo = jnp.exp(fresh_score - top)
    total = jnp.sum(expo, axis=2) + fresh_expo
    probs = (expo / total[:, :, None]).astype(jnp.bfloat16)
    fresh_prob = (fresh_expo / total).astype(jnp.bfloat16)
    o_latent = jnp.einsum("bhp,bpj->bhj", probs, cache_latent, preferred_element_type=jnp.float32)
    o_latent = (
        o_latent
        + fresh_prob.astype(jnp.float32)[:, :, None] * new_latent.astype(jnp.float32)[:, None, :]
    )
    return o_latent.astype(jnp.bfloat16)


def solution(mesh):
    n_dp = mesh.shape["dp"]
    chips = n_dp // 2
    swap = [(i, i ^ 1) for i in range(n_dp)]
    same_core = [[2 * c + k for c in range(chips)] for k in range(2)]

    def sibling(w):
        return lax.ppermute(w, "dp", swap)

    def exchange(v, split_axis=0):
        return lax.all_to_all(
            v, "dp", split_axis, 0, axis_index_groups=same_core, tiled=True
        )

    def summed(part, rows):
        got = exchange(part).reshape(chips, rows, part.shape[-1])
        return jnp.sum(got.astype(jnp.float32), axis=0)

    def dot(a, b):
        return jnp.dot(a, b, preferred_element_type=jnp.float32)

    def on_device(
        residual_in,
        q_latent,
        q_rope,
        cache_latent,
        cache_rope,
        new_latent,
        new_rope,
        lengths,
        counts,
        w_uv,
        w_o,
        norm_gain,
        w_gate,
        w_up,
        w_down,
    ):
        rows = residual_in.shape[0]
        core = lax.axis_index("dp") % 2
        w_uv2, w_o2 = sibling(w_uv), sibling(w_o)
        w_gate2, w_up2, w_down2 = sibling(w_gate), sibling(w_up), sibling(w_down)
        score_scale = (w_uv.shape[2] + q_rope.shape[1]) ** (-0.5)
        o_latent = attend(
            q_latent,
            q_rope,
            cache_latent,
            cache_rope,
            new_latent,
            new_rope,
            lengths,
            counts,
            score_scale,
        )
        by_head = exchange(o_latent, 1)
        heads = w_uv.shape[0]
        first = core == 0
        w_uv_pair = jnp.concatenate(
            [jnp.where(first, w_uv, w_uv2), jnp.where(first, w_uv2, w_uv)], axis=0
        )
        heads_v = jnp.einsum(
            "bhj,hjk->bhk", by_head, w_uv_pair, preferred_element_type=jnp.float32
        ).astype(jnp.bfloat16)
        flat = heads_v.reshape(heads_v.shape[0], -1)
        half = flat.shape[1] // 2
        mine = jnp.where(first, flat[:, :half], flat[:, half:])
        other = jnp.where(first, flat[:, half:], flat[:, :half])
        part = (dot(mine, w_o) + dot(other, w_o2)).astype(jnp.bfloat16)
        hidden_mine = residual_in.astype(jnp.float32) + summed(part, rows)
        normed_mine = normalize(hidden_mine, norm_gain)
        copies = jnp.broadcast_to(normed_mine[None], (chips,) + normed_mine.shape)
        normed = exchange(copies.reshape(chips * rows, -1))

        def activate(gate_w, up_w):
            return (jax.nn.silu(dot(normed, gate_w)) * dot(normed, up_w)).astype(jnp.bfloat16)

        part = (
            dot(activate(w_gate, w_up), w_down) + dot(activate(w_gate2, w_up2), w_down2)
        ).astype(jnp.bfloat16)
        return (hidden_mine + summed(part, rows)).astype(jnp.bfloat16)

    placed = (
        P(("rep", "dp"), None),
        P(("rep", "dp"), None, None),
        P(("rep", "dp"), None, None),
        P(("rep", "dp"), None, None),
        P(("rep", "dp"), None, None),
        P(("rep", "dp"), None),
        P(("rep", "dp"), None),
        P(("rep", "dp")),
        P(("rep", "dp")),
        P("dp", None, None),
        P("dp", None),
        P(),
        P(None, "dp"),
        P(None, "dp"),
        P("dp", None),
    )
    return jax.shard_map(
        on_device, mesh=mesh, in_specs=placed, out_specs=P(("rep", "dp"), None), check_vma=False
    )
```

```python
import jax
import jax.numpy as jnp
from jax import lax
from jax.experimental import pallas as pl
from jax.experimental.pallas import tpu as pltpu
from jax.sharding import PartitionSpec as P

F32, BF16 = jnp.float32, jnp.bfloat16
VMEM_BYTES = 40 * 2**20
HBM = pl.BlockSpec(memory_space=pl.ANY)
VMEM = pl.BlockSpec(memory_space=pltpu.VMEM)
SMEM = pl.BlockSpec(memory_space=pltpu.SMEM)


def normalize(values, gain):
    scaled = values * lax.rsqrt(jnp.mean(values * values, axis=-1, keepdims=True) + 1e-06)
    return (scaled * gain.astype(F32)).astype(BF16)


def mul(a, b, a_dim=1, b_dim=0):
    return lax.dot_general(a, b, (((a_dim,), (b_dim,)), ((), ())), preferred_element_type=F32)


def cost(flops, size):
    return pl.CostEstimate(flops=flops, bytes_accessed=size, transcendentals=0)


def attend_kernel(
    scale,
    lengths_ref,
    counts_ref,
    new_latent_ref,
    new_rope_ref,
    q_latent_hbm,
    q_rope_hbm,
    cache_latent_hbm,
    cache_rope_hbm,
    out_ref,
    q_lat,
    q_rot,
    c_lat,
    c_rot,
    acc,
    sems,
):
    rows, heads, width = q_lat.shape
    positions = c_lat.shape[1]
    pairs = (
        (q_latent_hbm, q_lat),
        (cache_latent_hbm, c_lat),
        (q_rope_hbm, q_rot),
        (cache_rope_hbm, c_rot),
    )
    copies = [
        [
            pltpu.make_async_copy(src.at[t], dst.at[t], sems.at[t, i])
            for i, (src, dst) in enumerate(pairs)
        ]
        for t in range(rows)
    ]
    for group in copies:
        for c in group:
            c.start()
    position = lax.broadcasted_iota(jnp.int32, (heads, positions), 1)
    fresh_lat = new_latent_ref[...]
    fresh_rot = new_rope_ref[...]
    for t in range(rows):
        for c in copies[t]:
            c.wait()
        used = jnp.where(t < counts_ref[0], lengths_ref[t], 0)
        q = q_lat[t]
        rot = q_rot[t].T
        keys = c_lat[t]
        scores = (mul(q, keys, 1, 1) + mul(rot, c_rot[t])) * scale
        fresh = ((mul(q, fresh_lat, 1, 1) + mul(rot, fresh_rot, 1, 1)) * scale)[:, t : t + 1]
        scores = jnp.where(position < used, scores, -jnp.inf)
        top = jnp.maximum(jnp.max(scores, axis=1, keepdims=True), fresh)
        expo = jnp.exp(scores - top)
        fresh_expo = jnp.exp(fresh - top)
        inverse = 1.0 / (jnp.sum(expo, axis=1, keepdims=True) + fresh_expo)
        probs = (expo * inverse).astype(BF16)
        fresh_prob = (fresh_expo * inverse).astype(BF16).astype(F32)
        o = mul(probs, keys) + fresh_prob * fresh_lat[t : t + 1].astype(F32)
        for j in range(width // 128):
            acc[j, pl.ds(t, heads, stride=rows), :] = o[:, j * 128 : (j + 1) * 128]
    for j in range(width // 128):
        out_ref[:, j * 128 : (j + 1) * 128] = acc[j].astype(BF16)


def attend(scale, q_latent, q_rope, cache_latent, cache_rope, new_latent, new_rope, lengths, counts):
    rows, heads, width = q_latent.shape
    positions = cache_latent.shape[1]

    def body(*refs):
        attend_kernel(scale, *refs)

    size = 2 * (q_latent.size * 2 + cache_latent.size + q_rope.size + cache_rope.size)
    flops = 4 * rows * heads * positions * width
    return pl.pallas_call(
        body,
        out_shape=jax.ShapeDtypeStruct((heads * rows, width), BF16),
        in_specs=[SMEM, SMEM, VMEM, VMEM, HBM, HBM, HBM, HBM],
        out_specs=VMEM,
        scratch_shapes=[
            pltpu.VMEM(q_latent.shape, BF16),
            pltpu.VMEM(q_rope.shape, BF16),
            pltpu.VMEM(cache_latent.shape, BF16),
            pltpu.VMEM(cache_rope.shape, BF16),
            pltpu.VMEM((width // 128, heads * rows, 128), F32),
            pltpu.SemaphoreType.DMA((rows, 4)),
        ],
        compiler_params=pltpu.CompilerParams(vmem_limit_bytes=VMEM_BYTES),
        cost_estimate=cost(flops, size),
        name="attend",
    )(lengths, counts, new_latent, new_rope, q_latent, q_rope, cache_latent, cache_rope)


def project_kernel(
    block,
    core_ref,
    got_hbm,
    uv_hbm,
    uv2_hbm,
    o_hbm,
    o2_hbm,
    out_ref,
    got,
    uv,
    uv2,
    wo,
    wo2,
    heads_v,
    sems,
):
    chips, span, width = got.shape
    heads = uv.shape[0]
    hv = uv.shape[2]
    rows = span // (2 * heads)
    cols = wo.shape[1]
    first = [
        pltpu.make_async_copy(src, dst, sems.at[i])
        for i, (src, dst) in enumerate(((got_hbm, got), (uv_hbm, uv), (uv2_hbm, uv2)))
    ]
    later = []
    for n in range(cols // block):
        at = pl.ds(n * block, block)
        later.append(
            [
                pltpu.make_async_copy(o_hbm.at[:, at], wo.at[:, at], sems.at[3 + 2 * n]),
                pltpu.make_async_copy(o2_hbm.at[:, at], wo2.at[:, at], sems.at[4 + 2 * n]),
            ]
        )
    for c in first:
        c.start()
    for group in later:
        for c in group:
            c.start()
    for c in first:
        c.wait()
    core = core_ref[0]
    half = heads * rows
    for s, w in enumerate((uv, uv2)):
        which = core if s == 0 else 1 - core
        mine = got[:, pl.ds(pl.multiple_of(which * half, half), half), :].astype(F32)
        for i in range(heads):
            x = mine[:, i * rows : (i + 1) * rows, :].reshape(chips * rows, width).astype(BF16)
            heads_v[s, :, i * hv : (i + 1) * hv] = mul(x, w[i]).astype(BF16)
    a, b = heads_v[0], heads_v[1]
    for n in range(cols // block):
        for c in later[n]:
            c.wait()
        at = slice(n * block, (n + 1) * block)
        out_ref[:, at] = (mul(a, wo[:, at]) + mul(b, wo2[:, at])).astype(BF16)


def project(core, got, w_uv, w_uv2, w_o, w_o2):
    chips, span, width = got.shape
    heads = w_uv.shape[0]
    rows = chips * span // (2 * heads)
    cols = w_o.shape[1]
    block = 512

    def body(*refs):
        project_kernel(block, *refs)

    size = 2 * (got.size + 2 * w_uv.size + 2 * w_o.size + rows * cols)
    return pl.pallas_call(
        body,
        out_shape=jax.ShapeDtypeStruct((rows, cols), BF16),
        in_specs=[SMEM, HBM, HBM, HBM, HBM, HBM],
        out_specs=VMEM,
        scratch_shapes=[
            pltpu.VMEM(got.shape, BF16),
            pltpu.VMEM(w_uv.shape, BF16),
            pltpu.VMEM(w_uv.shape, BF16),
            pltpu.VMEM(w_o.shape, BF16),
            pltpu.VMEM(w_o.shape, BF16),
            pltpu.VMEM((2, rows, w_o.shape[0]), BF16),
            pltpu.SemaphoreType.DMA((3 + 2 * (cols // block),)),
        ],
        compiler_params=pltpu.CompilerParams(vmem_limit_bytes=VMEM_BYTES),
        cost_estimate=cost(4 * rows * w_o.size, size),
        name="project",
    )(core, got, w_uv, w_uv2, w_o, w_o2)


def feed_kernel(block, x_ref, *refs):
    weights, (out_ref,), (scratch, sems) = refs[:6], refs[6:7], refs[7:]
    copies = [pltpu.make_async_copy(w, scratch.at[i], sems.at[i]) for i, w in enumerate(weights)]
    for c in copies:
        c.start()
    x = x_ref[...]
    activated = []
    for s in range(2):
        copies[2 * s].wait()
        gate = mul(x, scratch[2 * s], 1, 1)
        copies[2 * s + 1].wait()
        upper = mul(x, scratch[2 * s + 1], 1, 1)
        activated.append((gate / (1.0 + jnp.exp(-gate)) * upper).astype(BF16))
    copies[4].wait()
    copies[5].wait()
    cols = out_ref.shape[1]
    for n in range(cols // block):
        at = slice(n * block, (n + 1) * block)
        out_ref[:, at] = (
            mul(activated[0], scratch[4, :, at]) + mul(activated[1], scratch[5, :, at])
        ).astype(BF16)


def feed(x, *weights):
    rows, cols = x.shape

    def body(*refs):
        feed_kernel(512, *refs)

    size = 2 * (2 * x.size + sum(w.size for w in weights))
    return pl.pallas_call(
        body,
        out_shape=jax.ShapeDtypeStruct((rows, cols), BF16),
        in_specs=[VMEM] + [HBM] * 6,
        out_specs=VMEM,
        scratch_shapes=[
            pltpu.VMEM((6,) + weights[0].shape, BF16),
            pltpu.SemaphoreType.DMA((6,)),
        ],
        compiler_params=pltpu.CompilerParams(vmem_limit_bytes=VMEM_BYTES),
        cost_estimate=cost(12 * rows * weights[0].size, size),
        name="feed",
    )(x, *weights)


def solution(mesh):
    n_dp = mesh.shape["dp"]
    chips = n_dp // 2
    swap = [(i, i ^ 1) for i in range(n_dp)]
    same_core = [[2 * c + k for c in range(chips)] for k in range(2)]

    def sibling(w):
        return lax.ppermute(w, "dp", swap)

    def exchange(v):
        return lax.all_to_all(v, "dp", 0, 0, axis_index_groups=same_core, tiled=True)

    def summed(part, rows):
        got = exchange(part).reshape(chips, rows, part.shape[-1])
        return jnp.sum(got.astype(F32), axis=0)

    def on_device(
        residual_in,
        q_latent,
        q_rope,
        cache_latent,
        cache_rope,
        new_latent,
        new_rope,
        lengths,
        counts,
        w_uv,
        w_o,
        norm_gain,
        w_gate,
        w_up,
        w_down,
    ):
        rows = residual_in.shape[0]
        core = (lax.axis_index("dp") % 2).astype(jnp.int32).reshape(1)
        gate_t, up_t = w_gate.T, w_up.T
        w_uv2, w_o2 = sibling(w_uv), sibling(w_o)
        gate2, up2, down2 = sibling(gate_t), sibling(up_t), sibling(w_down)
        scale = (w_uv.shape[2] + q_rope.shape[1]) ** (-0.5)
        o_latent = attend(
            scale, q_latent, q_rope, cache_latent, cache_rope, new_latent, new_rope, lengths, counts
        )
        got = exchange(o_latent).reshape(chips, -1, o_latent.shape[1])
        part = project(core, got, w_uv, w_uv2, w_o, w_o2)
        hidden_mine = residual_in.astype(F32) + summed(part, rows)
        normed_mine = normalize(hidden_mine, norm_gain)
        copies = jnp.broadcast_to(normed_mine[None], (chips,) + normed_mine.shape)
        normed = exchange(copies.reshape(chips * rows, -1))
        part = feed(normed, gate_t, up_t, gate2, up2, w_down, down2)
        return (hidden_mine + summed(part, rows)).astype(BF16)

    placed = (
        P(("rep", "dp"), None),
        P(("rep", "dp"), None, None),
        P(("rep", "dp"), None, None),
        P(("rep", "dp"), None, None),
        P(("rep", "dp"), None, None),
        P(("rep", "dp"), None),
        P(("rep", "dp"), None),
        P(("rep", "dp")),
        P(("rep", "dp")),
        P("dp", None, None),
        P("dp", None),
        P(),
        P(None, "dp"),
        P(None, "dp"),
        P("dp", None),
    )
    return jax.shard_map(
        on_device, mesh=mesh, in_specs=placed, out_specs=P(("rep", "dp"), None), check_vma=False
    )
```

```python
import jax
import jax.numpy as jnp
from jax import lax
from jax.experimental import pallas as pl
from jax.experimental.pallas import tpu as pltpu
from jax.sharding import PartitionSpec as P

F32, BF16 = jnp.float32, jnp.bfloat16
VMEM_BYTES = 60 * 2**20
IN_FLIGHT = 8
ROOMY_BYTES = 52 * 2**20
HBM = pl.BlockSpec(memory_space=pltpu.HBM)
VMEM = pl.BlockSpec(memory_space=pltpu.VMEM)
SMEM = pl.BlockSpec(memory_space=pltpu.SMEM)


def normalize(values, gain):
    scaled = values * lax.rsqrt(jnp.mean(values * values, axis=-1, keepdims=True) + 1e-06)
    return (scaled * gain.astype(F32)).astype(BF16)


def mul(a, b, a_dim=1, b_dim=0):
    return lax.dot_general(a, b, (((a_dim,), (b_dim,)), ((), ())), preferred_element_type=F32)


def cost(flops, size):
    return pl.CostEstimate(flops=flops, bytes_accessed=size, transcendentals=0)


class Stream:
    def __init__(self, copies, window):
        self.copies, self.started, self.done = copies, 0, 0
        self.window = window
        self.fill()

    def fill(self):
        while self.started < min(len(self.copies), self.done + self.window):
            self.copies[self.started].start()
            self.started += 1

    def need(self, count):
        while self.done < count:
            self.copies[self.done].wait()
            self.done += 1
            self.fill()


def attend_kernel(
    scale,
    lengths_hbm,
    counts_hbm,
    new_latent_hbm,
    new_rope_hbm,
    q_latent_hbm,
    q_rope_hbm,
    cache_latent_hbm,
    cache_rope_hbm,
    out_ref,
    lengths,
    counts,
    n_lat,
    n_rot,
    q_lat,
    q_rot,
    c_lat,
    c_rot,
    scores,
    acc,
    sems,
):
    rows, heads, width = q_lat.shape
    positions = c_lat.shape[1]
    step = 2
    whole = (
        (lengths_hbm, lengths),
        (counts_hbm, counts),
        (new_latent_hbm, n_lat),
        (new_rope_hbm, n_rot),
        (q_rope_hbm, q_rot),
        (cache_rope_hbm, c_rot),
    )
    copies = [pltpu.make_async_copy(src, dst, sems.at[i]) for i, (src, dst) in enumerate(whole)]
    for g in range(rows // step):
        at = pl.ds(g * step, step)
        for src, dst in ((q_latent_hbm, q_lat), (cache_latent_hbm, c_lat)):
            copies.append(pltpu.make_async_copy(src.at[at], dst.at[at], sems.at[len(copies)]))
    stream = Stream(copies, len(whole) + 4)
    stream.need(len(whole))
    position = lax.broadcasted_iota(jnp.int32, (heads, positions), 1)
    fresh_lat = n_lat[...]
    fresh_rot = n_rot[...]
    fresh = []
    for t in range(rows):
        stream.need(len(whole) + 2 * (t // step + 1))
        used = jnp.where(t < counts[0], lengths[t], 0)
        q = q_lat[t]
        rot = q_rot[t].T
        part = (mul(q, c_lat[t], 1, 1) + mul(rot, c_rot[t])) * scale
        scores[t] = jnp.where(position < used, part, -jnp.inf)
        both = (mul(q, fresh_lat, 1, 1) + mul(rot, fresh_rot, 1, 1)) * scale
        fresh.append(both[:, t : t + 1])
    for t in range(rows):
        part = scores[t]
        top = jnp.maximum(jnp.max(part, axis=1, keepdims=True), fresh[t])
        expo = jnp.exp(part - top)
        fresh_expo = jnp.exp(fresh[t] - top)
        inverse = 1.0 / (jnp.sum(expo, axis=1, keepdims=True) + fresh_expo)
        probs = (expo * inverse).astype(BF16)
        fresh_prob = (fresh_expo * inverse).astype(BF16).astype(F32)
        o = mul(probs, c_lat[t]) + fresh_prob * fresh_lat[t : t + 1].astype(F32)
        for j in range(width // 128):
            acc[j, pl.ds(t, heads, stride=rows), :] = o[:, j * 128 : (j + 1) * 128]
    for j in range(width // 128):
        out_ref[:, j * 128 : (j + 1) * 128] = acc[j].astype(BF16)


def attend(scale, q_latent, q_rope, cache_latent, cache_rope, new_latent, new_rope, lengths, counts):
    rows, heads, width = q_latent.shape
    positions = cache_latent.shape[1]

    def body(*refs):
        attend_kernel(scale, *refs)

    size = 2 * (q_latent.size * 2 + cache_latent.size + q_rope.size + cache_rope.size)
    flops = 4 * rows * heads * positions * width
    return pl.pallas_call(
        body,
        out_shape=jax.ShapeDtypeStruct((heads * rows, width), BF16),
        in_specs=[HBM] * 8,
        out_specs=VMEM,
        scratch_shapes=[
            pltpu.SMEM(lengths.shape, jnp.int32),
            pltpu.SMEM(counts.shape, jnp.int32),
            pltpu.VMEM(new_latent.shape, BF16),
            pltpu.VMEM(new_rope.shape, BF16),
            pltpu.VMEM(q_latent.shape, BF16),
            pltpu.VMEM(q_rope.shape, BF16),
            pltpu.VMEM(cache_latent.shape, BF16),
            pltpu.VMEM(cache_rope.shape, BF16),
            pltpu.VMEM((rows, heads, positions), F32),
            pltpu.VMEM((width // 128, heads * rows, 128), F32),
            pltpu.SemaphoreType.DMA((6 + rows,)),
        ],
        compiler_params=pltpu.CompilerParams(vmem_limit_bytes=VMEM_BYTES),
        cost_estimate=cost(flops, size),
        name="attend",
    )(lengths, counts, new_latent, new_rope, q_latent, q_rope, cache_latent, cache_rope)


def send_out(out, out_hbm, n, block, sems, base):
    at = pl.ds(n * block, block)
    leave = pltpu.make_async_copy(out.at[:, at], out_hbm.at[:, at], sems.at[base + n])
    leave.start()
    return leave


def project_kernel(
    block, core_ref, got_hbm, uv1_hbm, uv2_hbm, wo1_hbm, wo2_hbm, out_hbm, got, uv, wo, heads_v, out, sems
):
    chips, span, width = got.shape
    heads, _, hv = uv1_hbm.shape
    rows = span // (2 * heads)
    depth, cols = wo1_hbm.shape
    copies = [pltpu.make_async_copy(got_hbm, got, sems.at[0])]
    for i, src in enumerate((uv1_hbm, uv2_hbm)):
        to = uv.at[pl.ds(i * heads, heads)]
        copies.append(pltpu.make_async_copy(src, to, sems.at[len(copies)]))
    for n in range(cols // block):
        at = pl.ds(n * block, block)
        for i, src in enumerate((wo1_hbm, wo2_hbm)):
            to = wo.at[pl.ds(i * depth, depth), at]
            copies.append(pltpu.make_async_copy(src.at[:, at], to, sems.at[len(copies)]))
    stream = Stream(copies, IN_FLIGHT + 3)
    stream.need(1)
    core = core_ref[0]
    half = heads * rows
    for s in range(2):
        which = core if s == 0 else 1 - core
        mine = got[:, pl.ds(pl.multiple_of(which * half, half), half), :].astype(F32)
        stream.need(s + 2)
        for i in range(heads):
            x = mine[:, i * rows : (i + 1) * rows, :].reshape(chips * rows, width).astype(BF16)
            n = s * heads + i
            heads_v[:, n * hv : (n + 1) * hv] = mul(x, uv[n]).astype(BF16)
    x = heads_v[...]
    leaving = []
    for n in range(cols // block):
        stream.need(3 + 2 * (n + 1))
        at = slice(n * block, (n + 1) * block)
        out[:, at] = mul(x, wo[:, at]).astype(BF16)
        leaving.append(send_out(out, out_hbm, n, block, sems, len(copies)))
    for c in leaving:
        c.wait()


def project(core, got, w_uv, w_uv2, w_o, w_o2):
    chips, span, width = got.shape
    heads, _, hv = w_uv.shape
    rows = chips * span // (2 * heads)
    depth, cols = w_o.shape
    block = 512

    def body(*refs):
        project_kernel(block, *refs)

    size = 2 * (got.size + 2 * w_uv.size + 2 * w_o.size + rows * cols)
    return pl.pallas_call(
        body,
        out_shape=jax.ShapeDtypeStruct((rows, cols), BF16),
        in_specs=[SMEM, HBM, HBM, HBM, HBM, HBM],
        out_specs=HBM,
        scratch_shapes=[
            pltpu.VMEM(got.shape, BF16),
            pltpu.VMEM((2 * heads, width, hv), BF16),
            pltpu.VMEM((2 * depth, cols), BF16),
            pltpu.VMEM((rows, 2 * depth), BF16),
            pltpu.VMEM((rows, cols), BF16),
            pltpu.SemaphoreType.DMA((3 + 3 * (cols // block),)),
        ],
        compiler_params=pltpu.CompilerParams(vmem_limit_bytes=ROOMY_BYTES),
        cost_estimate=cost(4 * rows * w_o.size, size),
        name="project",
    )(core, got, w_uv, w_uv2, w_o, w_o2)


def spans(first, size, total):
    edges = [0] + list(range(first, total, size)) + [total]
    return list(zip(edges[:-1], edges[1:]))


def feed_kernel(
    pieces, piece, block, x_ref, gate1, up1, gate2, up2, down1, down2, out_ref, gate_w, up_w, down_w, act, sems
):
    hidden, width = gate1.shape
    count = 0

    def copy(src, dst, rows, to, cols):
        nonlocal count
        count += 1
        return pltpu.make_async_copy(
            src.at[rows, cols], dst.at[to, cols], sems.at[count - 1]
        )

    everything = pl.ds(0, width)
    copies, ready = [], []
    for lo, hi in pieces:
        for dst, pair in ((gate_w, (gate1, gate2)), (up_w, (up1, up2))):
            for core, src in enumerate(pair):
                a, b = max(lo, core * hidden), min(hi, (core + 1) * hidden)
                for c in range(a, b, piece):
                    size = min(piece, b - c)
                    rows = pl.ds(c - core * hidden, size)
                    copies.append(copy(src, dst, rows, pl.ds(c, size), everything))
        ready.append(len(copies))
    for n in range(width // block):
        cols = pl.ds(n * block, block)
        for core, src in enumerate((down1, down2)):
            rows, to = pl.ds(0, hidden), pl.ds(core * hidden, hidden)
            copies.append(copy(src, down_w, rows, to, cols))
    stream = Stream(copies, IN_FLIGHT)
    x = x_ref[...]
    for (lo, hi), count in zip(pieces, ready):
        stream.need(count)
        gate = mul(x, gate_w[lo:hi], 1, 1)
        upper = mul(x, up_w[lo:hi], 1, 1)
        act[:, lo:hi] = (gate / (1.0 + jnp.exp(-gate)) * upper).astype(BF16)
    activated = act[...]
    for n in range(width // block):
        stream.need(ready[-1] + 2 * (n + 1))
        at = slice(n * block, (n + 1) * block)
        out_ref[:, at] = mul(activated, down_w[:, at]).astype(BF16)


def feed(x, *weights):
    rows, width = x.shape
    hidden = weights[0].shape[0]
    block = 512
    pieces = spans(256, 256, 2 * hidden)

    def body(*refs):
        feed_kernel(pieces, 96, block, *refs)

    size = 2 * (2 * x.size + sum(w.size for w in weights))
    return pl.pallas_call(
        body,
        out_shape=jax.ShapeDtypeStruct((rows, width), BF16),
        in_specs=[VMEM] + [HBM] * 6,
        out_specs=VMEM,
        scratch_shapes=[pltpu.VMEM((2 * hidden, width), BF16)] * 3
        + [
            pltpu.VMEM((rows, 2 * hidden), BF16),
            pltpu.SemaphoreType.DMA((48,)),
        ],
        compiler_params=pltpu.CompilerParams(vmem_limit_bytes=ROOMY_BYTES),
        cost_estimate=cost(12 * rows * weights[0].size, size),
        name="feed",
    )(x, *weights)


def solution(mesh):
    n_dp = mesh.shape["dp"]
    chips = n_dp // 2
    swap = [(i, i ^ 1) for i in range(n_dp)]
    same_core = [[2 * c + k for c in range(chips)] for k in range(2)]

    def sibling(w):
        return lax.ppermute(w, "dp", swap)

    def exchange(v):
        return lax.all_to_all(v, "dp", 0, 0, axis_index_groups=same_core, tiled=True)

    def summed(part, rows):
        got = exchange(part).reshape(chips, rows, part.shape[-1])
        return jnp.sum(got.astype(F32), axis=0)

    def on_device(
        residual_in,
        q_latent,
        q_rope,
        cache_latent,
        cache_rope,
        new_latent,
        new_rope,
        lengths,
        counts,
        w_uv,
        w_o,
        norm_gain,
        w_gate,
        w_up,
        w_down,
    ):
        rows = residual_in.shape[0]
        core = (lax.axis_index("dp") & 1).astype(jnp.int32).reshape(1)
        gate_t, up_t = w_gate.T, w_up.T
        w_uv2, w_o2 = sibling(w_uv), sibling(w_o)
        gate2, up2, down2 = sibling(gate_t), sibling(up_t), sibling(w_down)
        scale = (w_uv.shape[2] + q_rope.shape[1]) ** (-0.5)
        o_latent = attend(
            scale, q_latent, q_rope, cache_latent, cache_rope, new_latent, new_rope, lengths, counts
        )
        got = exchange(o_latent).reshape(chips, -1, o_latent.shape[1])
        part = project(core, got, w_uv, w_uv2, w_o, w_o2)
        hidden_mine = residual_in.astype(F32) + summed(part, rows)
        normed_mine = normalize(hidden_mine, norm_gain)
        copies = jnp.broadcast_to(normed_mine[None], (chips,) + normed_mine.shape)
        normed = exchange(copies.reshape(chips * rows, -1))
        part = feed(normed, gate_t, up_t, gate2, up2, w_down, down2)
        return (hidden_mine + summed(part, rows)).astype(BF16)

    placed = (
        P(("rep", "dp"), None),
        P(("rep", "dp"), None, None),
        P(("rep", "dp"), None, None),
        P(("rep", "dp"), None, None),
        P(("rep", "dp"), None, None),
        P(("rep", "dp"), None),
        P(("rep", "dp"), None),
        P(("rep", "dp")),
        P(("rep", "dp")),
        P("dp", None, None),
        P("dp", None),
        P(),
        P(None, "dp"),
        P(None, "dp"),
        P("dp", None),
    )
    return jax.shard_map(
        on_device, mesh=mesh, in_specs=placed, out_specs=P(("rep", "dp"), None), check_vma=False
    )
```

```python
import jax
import jax.numpy as jnp
from jax import lax
from jax.experimental import pallas as pl
from jax.experimental.pallas import tpu as pltpu
from jax.sharding import PartitionSpec as P

F32, BF16 = jnp.float32, jnp.bfloat16
VMEM_BYTES = 60 * 2**20
IN_FLIGHT = 12
ATTEND_GROUPS = ((0, 2), (2, 8))
ROOMY_BYTES = 52 * 2**20
HBM = pl.BlockSpec(memory_space=pltpu.HBM)
VMEM = pl.BlockSpec(memory_space=pltpu.VMEM)
SMEM = pl.BlockSpec(memory_space=pltpu.SMEM)


def normalize(values, gain):
    scaled = values * lax.rsqrt(jnp.mean(values * values, axis=-1, keepdims=True) + 1e-06)
    return (scaled * gain.astype(F32)).astype(BF16)


def mul(a, b, a_dim=1, b_dim=0):
    return lax.dot_general(a, b, (((a_dim,), (b_dim,)), ((), ())), preferred_element_type=F32)


def cost(flops, size):
    return pl.CostEstimate(flops=flops, bytes_accessed=size, transcendentals=0)


class Stream:
    def __init__(self, copies, window):
        self.copies, self.started, self.done = copies, 0, 0
        self.window = window
        self.fill()

    def fill(self):
        while self.started < min(len(self.copies), self.done + self.window):
            self.copies[self.started].start()
            self.started += 1

    def need(self, count):
        while self.done < count:
            self.copies[self.done].wait()
            self.done += 1
            self.fill()


def send_out(out, out_hbm, n, block, sems, base):
    at = pl.ds(n * block, block)
    leave = pltpu.make_async_copy(out.at[:, at], out_hbm.at[:, at], sems.at[base + n])
    leave.start()
    return leave


def attend_kernel(
    scale,
    lengths_hbm,
    counts_hbm,
    new_latent_hbm,
    new_rope_hbm,
    q_latent_hbm,
    q_rope_hbm,
    cache_latent_hbm,
    cache_rope_hbm,
    out_hbm,
    lengths,
    counts,
    n_lat,
    n_rot,
    q_lat,
    q_rot,
    c_lat,
    c_rot,
    scores,
    acc,
    out,
    sems,
):
    rows, heads, width = q_lat.shape
    positions = c_lat.shape[1]
    step = 2
    whole = (
        (lengths_hbm, lengths),
        (counts_hbm, counts),
        (new_latent_hbm, n_lat),
        (new_rope_hbm, n_rot),
        (q_rope_hbm, q_rot),
        (cache_rope_hbm, c_rot),
    )
    copies = [pltpu.make_async_copy(src, dst, sems.at[i]) for i, (src, dst) in enumerate(whole)]
    for g in range(rows // step):
        at = pl.ds(g * step, step)
        for src, dst in ((q_latent_hbm, q_lat), (cache_latent_hbm, c_lat)):
            copies.append(pltpu.make_async_copy(src.at[at], dst.at[at], sems.at[len(copies)]))
    stream = Stream(copies, len(whole) + 4)
    stream.need(len(whole))
    position = lax.broadcasted_iota(jnp.int32, (heads, positions), 1)
    fresh_lat = n_lat[...]
    fresh_rot = n_rot[...]
    for begin, end in ATTEND_GROUPS:
        stream.need(len(whole) + 2 * (end // step))
        fresh = []
        for t in range(begin, end):
            used = jnp.where(t < counts[0], lengths[t], 0)
            q = q_lat[t]
            rot = q_rot[t].T
            part = (mul(q, c_lat[t], 1, 1) + mul(rot, c_rot[t])) * scale
            scores[t] = jnp.where(position < used, part, -jnp.inf)
            both = (mul(q, fresh_lat, 1, 1) + mul(rot, fresh_rot, 1, 1)) * scale
            fresh.append(both[:, t : t + 1])
        for t in range(begin, end):
            part = scores[t]
            new = fresh[t - begin]
            top = jnp.maximum(jnp.max(part, axis=1, keepdims=True), new)
            expo = jnp.exp(part - top)
            fresh_expo = jnp.exp(new - top)
            inverse = 1.0 / (jnp.sum(expo, axis=1, keepdims=True) + fresh_expo)
            probs = (expo * inverse).astype(BF16)
            fresh_prob = (fresh_expo * inverse).astype(BF16).astype(F32)
            o = mul(probs, c_lat[t]) + fresh_prob * fresh_lat[t : t + 1].astype(F32)
            for j in range(width // 128):
                acc[j, pl.ds(t, heads, stride=rows), :] = o[:, j * 128 : (j + 1) * 128]
    leaving = []
    for j in range(width // 128):
        out[:, j * 128 : (j + 1) * 128] = acc[j].astype(BF16)
        leaving.append(send_out(out, out_hbm, j, 128, sems, len(copies)))
    for c in leaving:
        c.wait()


def attend(scale, q_latent, q_rope, cache_latent, cache_rope, new_latent, new_rope, lengths, counts):
    rows, heads, width = q_latent.shape
    positions = cache_latent.shape[1]

    def body(*refs):
        attend_kernel(scale, *refs)

    size = 2 * (q_latent.size * 2 + cache_latent.size + q_rope.size + cache_rope.size)
    flops = 4 * rows * heads * positions * width
    return pl.pallas_call(
        body,
        out_shape=jax.ShapeDtypeStruct((heads * rows, width), BF16),
        in_specs=[HBM] * 8,
        out_specs=HBM,
        scratch_shapes=[
            pltpu.SMEM(lengths.shape, jnp.int32),
            pltpu.SMEM(counts.shape, jnp.int32),
            pltpu.VMEM(new_latent.shape, BF16),
            pltpu.VMEM(new_rope.shape, BF16),
            pltpu.VMEM(q_latent.shape, BF16),
            pltpu.VMEM(q_rope.shape, BF16),
            pltpu.VMEM(cache_latent.shape, BF16),
            pltpu.VMEM(cache_rope.shape, BF16),
            pltpu.VMEM((rows, heads, positions), F32),
            pltpu.VMEM((width // 128, heads * rows, 128), F32),
            pltpu.VMEM((heads * rows, width), BF16),
            pltpu.SemaphoreType.DMA((6 + rows + width // 128,)),
        ],
        compiler_params=pltpu.CompilerParams(vmem_limit_bytes=VMEM_BYTES),
        cost_estimate=cost(flops, size),
        name="attend",
    )(lengths, counts, new_latent, new_rope, q_latent, q_rope, cache_latent, cache_rope)


def project_kernel(
    block, core_ref, got_hbm, uv1_hbm, uv2_hbm, wo1_hbm, wo2_hbm, out_hbm, got, uv, wo, heads_v, out, sems
):
    chips, span, width = got.shape
    heads, _, hv = uv1_hbm.shape
    rows = span // (2 * heads)
    depth, cols = wo1_hbm.shape
    copies = [pltpu.make_async_copy(got_hbm, got, sems.at[0])]
    for i, src in enumerate((uv1_hbm, uv2_hbm)):
        to = uv.at[pl.ds(i * heads, heads)]
        copies.append(pltpu.make_async_copy(src, to, sems.at[len(copies)]))
    for n in range(cols // block):
        at = pl.ds(n * block, block)
        for i, src in enumerate((wo1_hbm, wo2_hbm)):
            to = wo.at[pl.ds(i * depth, depth), at]
            copies.append(pltpu.make_async_copy(src.at[:, at], to, sems.at[len(copies)]))
    stream = Stream(copies, IN_FLIGHT + 3)
    stream.need(1)
    core = core_ref[0]
    half = heads * rows
    for s in range(2):
        which = core if s == 0 else 1 - core
        mine = got[:, pl.ds(pl.multiple_of(which * half, half), half), :].astype(F32)
        stream.need(s + 2)
        for i in range(heads):
            x = mine[:, i * rows : (i + 1) * rows, :].reshape(chips * rows, width).astype(BF16)
            n = s * heads + i
            heads_v[:, n * hv : (n + 1) * hv] = mul(x, uv[n]).astype(BF16)
    x = heads_v[...]
    leaving = []
    for n in range(cols // block):
        stream.need(3 + 2 * (n + 1))
        at = slice(n * block, (n + 1) * block)
        out[:, at] = mul(x, wo[:, at]).astype(BF16)
        leaving.append(send_out(out, out_hbm, n, block, sems, len(copies)))
    for c in leaving:
        c.wait()


def project(core, got, w_uv, w_uv2, w_o, w_o2):
    chips, span, width = got.shape
    heads, _, hv = w_uv.shape
    rows = chips * span // (2 * heads)
    depth, cols = w_o.shape
    block = 896

    def body(*refs):
        project_kernel(block, *refs)

    size = 2 * (got.size + 2 * w_uv.size + 2 * w_o.size + rows * cols)
    return pl.pallas_call(
        body,
        out_shape=jax.ShapeDtypeStruct((rows, cols), BF16),
        in_specs=[SMEM, HBM, HBM, HBM, HBM, HBM],
        out_specs=HBM,
        scratch_shapes=[
            pltpu.VMEM(got.shape, BF16),
            pltpu.VMEM((2 * heads, width, hv), BF16),
            pltpu.VMEM((2 * depth, cols), BF16),
            pltpu.VMEM((rows, 2 * depth), BF16),
            pltpu.VMEM((rows, cols), BF16),
            pltpu.SemaphoreType.DMA((3 + 3 * (cols // block),)),
        ],
        compiler_params=pltpu.CompilerParams(vmem_limit_bytes=ROOMY_BYTES),
        cost_estimate=cost(4 * rows * w_o.size, size),
        name="project",
    )(core, got, w_uv, w_uv2, w_o, w_o2)


def spans(first, size, total):
    edges = [0] + list(range(first, total, size)) + [total]
    return list(zip(edges[:-1], edges[1:]))


def feed_kernel(
    pieces, piece, block, x_ref, gate1, up1, gate2, up2, down1, down2, out_ref, gate_w, up_w, down_w, act, sems
):
    hidden, width = gate1.shape
    count = 0

    def copy(src, dst, rows, to, cols):
        nonlocal count
        count += 1
        return pltpu.make_async_copy(
            src.at[rows, cols], dst.at[to, cols], sems.at[count - 1]
        )

    everything = pl.ds(0, width)
    copies, ready = [], []
    for lo, hi in pieces:
        for dst, pair in ((gate_w, (gate1, gate2)), (up_w, (up1, up2))):
            for core, src in enumerate(pair):
                a, b = max(lo, core * hidden), min(hi, (core + 1) * hidden)
                for c in range(a, b, piece):
                    size = min(piece, b - c)
                    rows = pl.ds(c - core * hidden, size)
                    copies.append(copy(src, dst, rows, pl.ds(c, size), everything))
        ready.append(len(copies))
    for n in range(width // block):
        cols = pl.ds(n * block, block)
        for core, src in enumerate((down1, down2)):
            rows, to = pl.ds(0, hidden), pl.ds(core * hidden, hidden)
            copies.append(copy(src, down_w, rows, to, cols))
    stream = Stream(copies, IN_FLIGHT)
    x = x_ref[...]
    for (lo, hi), count in zip(pieces, ready):
        stream.need(count)
        gate = mul(x, gate_w[lo:hi], 1, 1)
        upper = mul(x, up_w[lo:hi], 1, 1)
        act[:, lo:hi] = (gate / (1.0 + jnp.exp(-gate)) * upper).astype(BF16)
    activated = act[...]
    for n in range(width // block):
        stream.need(ready[-1] + 2 * (n + 1))
        at = slice(n * block, (n + 1) * block)
        out_ref[:, at] = mul(activated, down_w[:, at]).astype(BF16)


def feed(x, *weights):
    rows, width = x.shape
    hidden = weights[0].shape[0]
    block = 512
    pieces = spans(128, 256, 2 * hidden)

    def body(*refs):
        feed_kernel(pieces, 96, block, *refs)

    size = 2 * (2 * x.size + sum(w.size for w in weights))
    return pl.pallas_call(
        body,
        out_shape=jax.ShapeDtypeStruct((rows, width), BF16),
        in_specs=[VMEM] + [HBM] * 6,
        out_specs=VMEM,
        scratch_shapes=[pltpu.VMEM((2 * hidden, width), BF16)] * 3
        + [
            pltpu.VMEM((rows, 2 * hidden), BF16),
            pltpu.SemaphoreType.DMA((48,)),
        ],
        compiler_params=pltpu.CompilerParams(vmem_limit_bytes=ROOMY_BYTES),
        cost_estimate=cost(12 * rows * weights[0].size, size),
        name="feed",
    )(x, *weights)


def solution(mesh):
    n_dp = mesh.shape["dp"]
    chips = n_dp // 2
    swap = [(i, i ^ 1) for i in range(n_dp)]
    same_core = [[2 * c + k for c in range(chips)] for k in range(2)]

    def sibling(w):
        return lax.ppermute(w, "dp", swap)

    def exchange(v):
        return lax.all_to_all(v, "dp", 0, 0, axis_index_groups=same_core, tiled=True)

    def summed(part, rows):
        got = exchange(part).reshape(chips, rows, part.shape[-1])
        return jnp.sum(got.astype(F32), axis=0)

    def on_device(
        residual_in,
        q_latent,
        q_rope,
        cache_latent,
        cache_rope,
        new_latent,
        new_rope,
        lengths,
        counts,
        w_uv,
        w_o,
        norm_gain,
        w_gate,
        w_up,
        w_down,
    ):
        rows = residual_in.shape[0]
        core = (lax.axis_index("dp") & 1).astype(jnp.int32).reshape(1)
        gate_t, up_t = w_gate.T, w_up.T
        w_uv2, w_o2 = sibling(w_uv), sibling(w_o)
        gate2, up2, down2 = sibling(gate_t), sibling(up_t), sibling(w_down)
        scale = (w_uv.shape[2] + q_rope.shape[1]) ** (-0.5)
        o_latent = attend(
            scale, q_latent, q_rope, cache_latent, cache_rope, new_latent, new_rope, lengths, counts
        )
        got = exchange(o_latent).reshape(chips, -1, o_latent.shape[1])
        got, gate2, up2, down2 = lax.optimization_barrier((got, gate2, up2, down2))
        part = project(core, got, w_uv, w_uv2, w_o, w_o2)
        hidden_mine = residual_in.astype(F32) + summed(part, rows)
        normed_mine = normalize(hidden_mine, norm_gain)
        copies = jnp.broadcast_to(normed_mine[None], (chips,) + normed_mine.shape)
        normed = exchange(copies.reshape(chips * rows, -1))
        part = feed(normed, gate_t, up_t, gate2, up2, w_down, down2)
        return (hidden_mine + summed(part, rows)).astype(BF16)

    placed = (
        P(("rep", "dp"), None),
        P(("rep", "dp"), None, None),
        P(("rep", "dp"), None, None),
        P(("rep", "dp"), None, None),
        P(("rep", "dp"), None, None),
        P(("rep", "dp"), None),
        P(("rep", "dp"), None),
        P(("rep", "dp")),
        P(("rep", "dp")),
        P("dp", None, None),
        P("dp", None),
        P(),
        P(None, "dp"),
        P(None, "dp"),
        P("dp", None),
    )
    return jax.shard_map(
        on_device, mesh=mesh, in_specs=placed, out_specs=P(("rep", "dp"), None), check_vma=False
    )
```

```python
import jax
import jax.numpy as jnp
from jax import lax
from jax.experimental import pallas as pl
from jax.experimental.pallas import tpu as pltpu
from jax.sharding import PartitionSpec as P

F32, BF16 = jnp.float32, jnp.bfloat16
VMEM_BYTES = 60 * 2**20
IN_FLIGHT = 12
ATTEND_GROUPS = ((0, 2), (2, 8))
ROOMY_BYTES = 52 * 2**20
PROJECT_BYTES = 50 * 2**20
HBM = pl.BlockSpec(memory_space=pltpu.HBM)
VMEM = pl.BlockSpec(memory_space=pltpu.VMEM)
SMEM = pl.BlockSpec(memory_space=pltpu.SMEM)


def normalize(values, gain):
    scaled = values * lax.rsqrt(jnp.mean(values * values, axis=-1, keepdims=True) + 1e-06)
    return (scaled * gain.astype(F32)).astype(BF16)


def mul(a, b, a_dim=1, b_dim=0):
    return lax.dot_general(a, b, (((a_dim,), (b_dim,)), ((), ())), preferred_element_type=F32)


def cost(flops, size):
    return pl.CostEstimate(flops=flops, bytes_accessed=size, transcendentals=0)


class Stream:
    def __init__(self, copies, window):
        self.copies, self.started, self.done = copies, 0, 0
        self.window = window
        self.fill()

    def fill(self):
        while self.started < min(len(self.copies), self.done + self.window):
            self.copies[self.started].start()
            self.started += 1

    def need(self, count):
        while self.done < count:
            self.copies[self.done].wait()
            self.done += 1
            self.fill()


def send_out(out, out_hbm, n, block, sems, base):
    at = pl.ds(n * block, block)
    leave = pltpu.make_async_copy(out.at[:, at], out_hbm.at[:, at], sems.at[base + n])
    leave.start()
    return leave


def attend_kernel(
    scale,
    lengths_hbm,
    counts_hbm,
    new_latent_hbm,
    new_rope_hbm,
    q_latent_hbm,
    q_rope_hbm,
    cache_latent_hbm,
    cache_rope_hbm,
    out_hbm,
    lengths,
    counts,
    n_lat,
    n_rot,
    q_lat,
    q_rot,
    c_lat,
    c_rot,
    scores,
    acc,
    out,
    sems,
):
    rows, heads, width = q_lat.shape
    positions = c_lat.shape[1]
    step = 2
    whole = (
        (lengths_hbm, lengths),
        (counts_hbm, counts),
        (new_latent_hbm, n_lat),
        (new_rope_hbm, n_rot),
        (q_rope_hbm, q_rot),
        (cache_rope_hbm, c_rot),
    )
    copies = [pltpu.make_async_copy(src, dst, sems.at[i]) for i, (src, dst) in enumerate(whole)]
    for g in range(rows // step):
        at = pl.ds(g * step, step)
        for src, dst in ((q_latent_hbm, q_lat), (cache_latent_hbm, c_lat)):
            copies.append(pltpu.make_async_copy(src.at[at], dst.at[at], sems.at[len(copies)]))
    stream = Stream(copies, len(whole) + 4)
    stream.need(len(whole))
    position = lax.broadcasted_iota(jnp.int32, (heads, positions), 1)
    fresh_lat = n_lat[...]
    fresh_rot = n_rot[...]
    for begin, end in ATTEND_GROUPS:
        stream.need(len(whole) + 2 * (end // step))
        fresh = []
        for t in range(begin, end):
            used = jnp.where(t < counts[0], lengths[t], 0)
            q = q_lat[t]
            rot = q_rot[t].T
            part = (mul(q, c_lat[t], 1, 1) + mul(rot, c_rot[t])) * scale
            scores[t] = jnp.where(position < used, part, -jnp.inf)
            both = (mul(q, fresh_lat, 1, 1) + mul(rot, fresh_rot, 1, 1)) * scale
            fresh.append(both[:, t : t + 1])
        for t in range(begin, end):
            part = scores[t]
            new = fresh[t - begin]
            top = jnp.maximum(jnp.max(part, axis=1, keepdims=True), new)
            expo = jnp.exp(part - top)
            fresh_expo = jnp.exp(new - top)
            inverse = 1.0 / (jnp.sum(expo, axis=1, keepdims=True) + fresh_expo)
            probs = (expo * inverse).astype(BF16)
            fresh_prob = (fresh_expo * inverse).astype(BF16).astype(F32)
            o = mul(probs, c_lat[t]) + fresh_prob * fresh_lat[t : t + 1].astype(F32)
            for j in range(width // 128):
                acc[j, pl.ds(t, heads, stride=rows), :] = o[:, j * 128 : (j + 1) * 128]
    leaving = []
    for j in range(width // 128):
        out[:, j * 128 : (j + 1) * 128] = acc[j].astype(BF16)
        leaving.append(send_out(out, out_hbm, j, 128, sems, len(copies)))
    for c in leaving:
        c.wait()


def attend(scale, q_latent, q_rope, cache_latent, cache_rope, new_latent, new_rope, lengths, counts):
    rows, heads, width = q_latent.shape
    positions = cache_latent.shape[1]

    def body(*refs):
        attend_kernel(scale, *refs)

    size = 2 * (q_latent.size * 2 + cache_latent.size + q_rope.size + cache_rope.size)
    flops = 4 * rows * heads * positions * width
    return pl.pallas_call(
        body,
        out_shape=jax.ShapeDtypeStruct((heads * rows, width), BF16),
        in_specs=[HBM] * 8,
        out_specs=HBM,
        scratch_shapes=[
            pltpu.SMEM(lengths.shape, jnp.int32),
            pltpu.SMEM(counts.shape, jnp.int32),
            pltpu.VMEM(new_latent.shape, BF16),
            pltpu.VMEM(new_rope.shape, BF16),
            pltpu.VMEM(q_latent.shape, BF16),
            pltpu.VMEM(q_rope.shape, BF16),
            pltpu.VMEM(cache_latent.shape, BF16),
            pltpu.VMEM(cache_rope.shape, BF16),
            pltpu.VMEM((rows, heads, positions), F32),
            pltpu.VMEM((width // 128, heads * rows, 128), F32),
            pltpu.VMEM((heads * rows, width), BF16),
            pltpu.SemaphoreType.DMA((6 + rows + width // 128,)),
        ],
        compiler_params=pltpu.CompilerParams(vmem_limit_bytes=VMEM_BYTES),
        cost_estimate=cost(flops, size),
        name="attend",
    )(lengths, counts, new_latent, new_rope, q_latent, q_rope, cache_latent, cache_rope)


def project_kernel(
    block, core_ref, got_hbm, uv1_hbm, uv2_hbm, wo1_hbm, wo2_hbm, out_hbm, got, uv, wo, heads_v, out, sems
):
    chips, span, width = got.shape
    heads, _, hv = uv1_hbm.shape
    rows = span // (2 * heads)
    depth, cols = wo1_hbm.shape
    copies = [pltpu.make_async_copy(got_hbm, got, sems.at[0])]
    for i, src in enumerate((uv1_hbm, uv2_hbm)):
        to = uv.at[pl.ds(i * heads, heads)]
        copies.append(pltpu.make_async_copy(src, to, sems.at[len(copies)]))
    for n in range(cols // block):
        at = pl.ds(n * block, block)
        for i, src in enumerate((wo1_hbm, wo2_hbm)):
            to = wo.at[pl.ds(i * depth, depth), at]
            copies.append(pltpu.make_async_copy(src.at[:, at], to, sems.at[len(copies)]))
    stream = Stream(copies, IN_FLIGHT + 3)
    stream.need(1)
    core = core_ref[0]
    half = heads * rows
    for s in range(2):
        which = core if s == 0 else 1 - core
        mine = got[:, pl.ds(pl.multiple_of(which * half, half), half), :].astype(F32)
        stream.need(s + 2)
        for i in range(heads):
            x = mine[:, i * rows : (i + 1) * rows, :].reshape(chips * rows, width).astype(BF16)
            n = s * heads + i
            heads_v[:, n * hv : (n + 1) * hv] = mul(x, uv[n]).astype(BF16)
    x = heads_v[...]
    leaving = []
    for n in range(cols // block):
        stream.need(3 + 2 * (n + 1))
        at = slice(n * block, (n + 1) * block)
        out[:, at] = mul(x, wo[:, at]).astype(BF16)
        leaving.append(send_out(out, out_hbm, n, block, sems, len(copies)))
    for c in leaving:
        c.wait()


def project(core, got, w_uv, w_uv2, w_o, w_o2):
    chips, span, width = got.shape
    heads, _, hv = w_uv.shape
    rows = chips * span // (2 * heads)
    depth, cols = w_o.shape
    block = 896

    def body(*refs):
        project_kernel(block, *refs)

    size = 2 * (got.size + 2 * w_uv.size + 2 * w_o.size + rows * cols)
    return pl.pallas_call(
        body,
        out_shape=jax.ShapeDtypeStruct((rows, cols), BF16),
        in_specs=[SMEM, HBM, HBM, HBM, HBM, HBM],
        out_specs=HBM,
        scratch_shapes=[
            pltpu.VMEM(got.shape, BF16),
            pltpu.VMEM((2 * heads, width, hv), BF16),
            pltpu.VMEM((2 * depth, cols), BF16),
            pltpu.VMEM((rows, 2 * depth), BF16),
            pltpu.VMEM((rows, cols), BF16),
            pltpu.SemaphoreType.DMA((3 + 3 * (cols // block),)),
        ],
        compiler_params=pltpu.CompilerParams(vmem_limit_bytes=PROJECT_BYTES),
        cost_estimate=cost(4 * rows * w_o.size, size),
        name="project",
    )(core, got, w_uv, w_uv2, w_o, w_o2)


def spans(first, size, total):
    edges = [0] + list(range(first, total, size)) + [total]
    return list(zip(edges[:-1], edges[1:]))


def feed_kernel(
    pieces, piece, block, x_ref, gate1, up1, gate2, up2, down1, down2, out_ref, gate_w, up_w, down_w, act, sems
):
    hidden, width = gate1.shape
    count = 0

    def copy(src, dst, rows, to, cols):
        nonlocal count
        count += 1
        return pltpu.make_async_copy(
            src.at[rows, cols], dst.at[to, cols], sems.at[count - 1]
        )

    everything = pl.ds(0, width)
    copies, ready = [], []
    for lo, hi in pieces:
        for dst, pair in ((gate_w, (gate1, gate2)), (up_w, (up1, up2))):
            for core, src in enumerate(pair):
                a, b = max(lo, core * hidden), min(hi, (core + 1) * hidden)
                for c in range(a, b, piece):
                    size = min(piece, b - c)
                    rows = pl.ds(c - core * hidden, size)
                    copies.append(copy(src, dst, rows, pl.ds(c, size), everything))
        ready.append(len(copies))
    for n in range(width // block):
        cols = pl.ds(n * block, block)
        for core, src in enumerate((down1, down2)):
            rows, to = pl.ds(0, hidden), pl.ds(core * hidden, hidden)
            copies.append(copy(src, down_w, rows, to, cols))
    stream = Stream(copies, IN_FLIGHT)
    x = x_ref[...]
    for (lo, hi), count in zip(pieces, ready):
        stream.need(count)
        gate = mul(x, gate_w[lo:hi], 1, 1)
        upper = mul(x, up_w[lo:hi], 1, 1)
        act[:, lo:hi] = (gate / (1.0 + jnp.exp(-gate)) * upper).astype(BF16)
    activated = act[...]
    for n in range(width // block):
        stream.need(ready[-1] + 2 * (n + 1))
        at = slice(n * block, (n + 1) * block)
        out_ref[:, at] = mul(activated, down_w[:, at]).astype(BF16)


def feed(x, *weights):
    rows, width = x.shape
    hidden = weights[0].shape[0]
    block = 512
    pieces = spans(128, 256, 2 * hidden)

    def body(*refs):
        feed_kernel(pieces, 96, block, *refs)

    size = 2 * (2 * x.size + sum(w.size for w in weights))
    return pl.pallas_call(
        body,
        out_shape=jax.ShapeDtypeStruct((rows, width), BF16),
        in_specs=[VMEM] + [HBM] * 6,
        out_specs=VMEM,
        scratch_shapes=[pltpu.VMEM((2 * hidden, width), BF16)] * 3
        + [
            pltpu.VMEM((rows, 2 * hidden), BF16),
            pltpu.SemaphoreType.DMA((48,)),
        ],
        compiler_params=pltpu.CompilerParams(vmem_limit_bytes=ROOMY_BYTES),
        cost_estimate=cost(12 * rows * weights[0].size, size),
        name="feed",
    )(x, *weights)


def solution(mesh):
    n_dp = mesh.shape["dp"]
    chips = n_dp // 2
    swap = [(i, i ^ 1) for i in range(n_dp)]
    same_core = [[2 * c + k for c in range(chips)] for k in range(2)]

    def sibling(w):
        return lax.ppermute(w, "dp", swap)

    def exchange(v):
        return lax.all_to_all(v, "dp", 0, 0, axis_index_groups=same_core, tiled=True)

    def summed(part, rows):
        got = exchange(part).reshape(chips, rows, part.shape[-1])
        return jnp.sum(got.astype(F32), axis=0)

    def on_device(
        residual_in,
        q_latent,
        q_rope,
        cache_latent,
        cache_rope,
        new_latent,
        new_rope,
        lengths,
        counts,
        w_uv,
        w_o,
        norm_gain,
        w_gate,
        w_up,
        w_down,
    ):
        rows = residual_in.shape[0]
        core = (lax.axis_index("dp") & 1).astype(jnp.int32).reshape(1)
        gate_t, up_t = w_gate.T, w_up.T
        w_uv2, w_o2 = sibling(w_uv), sibling(w_o)
        gate2, up2, down2 = sibling(gate_t), sibling(up_t), sibling(w_down)
        scale = (w_uv.shape[2] + q_rope.shape[1]) ** (-0.5)
        o_latent = attend(
            scale, q_latent, q_rope, cache_latent, cache_rope, new_latent, new_rope, lengths, counts
        )
        got = exchange(o_latent).reshape(chips, -1, o_latent.shape[1])
        got, gate2, up2, down2 = lax.optimization_barrier((got, gate2, up2, down2))
        part = project(core, got, w_uv, w_uv2, w_o, w_o2)
        hidden_mine = residual_in.astype(F32) + summed(part, rows)
        normed_mine = normalize(hidden_mine, norm_gain)
        copies = jnp.broadcast_to(normed_mine[None], (chips,) + normed_mine.shape)
        normed = exchange(copies.reshape(chips * rows, -1))
        part = feed(normed, gate_t, up_t, gate2, up2, w_down, down2)
        return (hidden_mine + summed(part, rows)).astype(BF16)

    placed = (
        P(("rep", "dp"), None),
        P(("rep", "dp"), None, None),
        P(("rep", "dp"), None, None),
        P(("rep", "dp"), None, None),
        P(("rep", "dp"), None, None),
        P(("rep", "dp"), None),
        P(("rep", "dp"), None),
        P(("rep", "dp")),
        P(("rep", "dp")),
        P("dp", None, None),
        P("dp", None),
        P(),
        P(None, "dp"),
        P(None, "dp"),
        P("dp", None),
    )
    return jax.shard_map(
        on_device, mesh=mesh, in_specs=placed, out_specs=P(("rep", "dp"), None), check_vma=False
    )
```

```python
import jax
import jax.numpy as jnp
from jax import lax
from jax.experimental import pallas as pl
from jax.experimental.pallas import tpu as pltpu
from jax.sharding import PartitionSpec as P

F32, BF16 = jnp.float32, jnp.bfloat16
VMEM_BYTES = 60 * 2**20
IN_FLIGHT = 12
ATTEND_GROUPS = ((0, 2), (2, 8))
ROOMY_BYTES = 52 * 2**20
PROJECT_BYTES = 50 * 2**20
HBM = pl.BlockSpec(memory_space=pltpu.HBM)
VMEM = pl.BlockSpec(memory_space=pltpu.VMEM)
SMEM = pl.BlockSpec(memory_space=pltpu.SMEM)


def normalize(values, gain):
    scaled = values * lax.rsqrt(jnp.mean(values * values, axis=-1, keepdims=True) + 1e-06)
    return (scaled * gain.astype(F32)).astype(BF16)


def mul(a, b, a_dim=1, b_dim=0):
    return lax.dot_general(a, b, (((a_dim,), (b_dim,)), ((), ())), preferred_element_type=F32)


def cost(flops, size):
    return pl.CostEstimate(flops=flops, bytes_accessed=size, transcendentals=0)


class Stream:
    def __init__(self, copies, window):
        self.copies, self.started, self.done = copies, 0, 0
        self.window = window
        self.fill()

    def fill(self):
        while self.started < min(len(self.copies), self.done + self.window):
            self.copies[self.started].start()
            self.started += 1

    def need(self, count):
        while self.done < count:
            self.copies[self.done].wait()
            self.done += 1
            self.fill()


def send_out(out, out_hbm, n, block, sems, base):
    at = pl.ds(n * block, block)
    leave = pltpu.make_async_copy(out.at[:, at], out_hbm.at[:, at], sems.at[base + n])
    leave.start()
    return leave


def attend_kernel(
    scale,
    lengths_hbm,
    counts_hbm,
    new_latent_hbm,
    new_rope_hbm,
    q_latent_hbm,
    q_rope_hbm,
    cache_latent_hbm,
    cache_rope_hbm,
    out_hbm,
    lengths,
    counts,
    n_lat,
    n_rot,
    q_lat,
    q_rot,
    c_lat,
    c_rot,
    scores,
    acc,
    out,
    sems,
):
    rows, heads, width = q_lat.shape
    positions = c_lat.shape[1]
    step = 2
    whole = (
        (lengths_hbm, lengths),
        (counts_hbm, counts),
        (new_latent_hbm, n_lat),
        (new_rope_hbm, n_rot),
        (q_rope_hbm, q_rot),
        (cache_rope_hbm, c_rot),
    )
    copies = [pltpu.make_async_copy(src, dst, sems.at[i]) for i, (src, dst) in enumerate(whole)]
    for g in range(rows // step):
        at = pl.ds(g * step, step)
        for src, dst in ((q_latent_hbm, q_lat), (cache_latent_hbm, c_lat)):
            copies.append(pltpu.make_async_copy(src.at[at], dst.at[at], sems.at[len(copies)]))
    stream = Stream(copies, len(whole) + 4)
    stream.need(len(whole))
    position = lax.broadcasted_iota(jnp.int32, (heads, positions), 1)
    fresh_lat = n_lat[...]
    fresh_rot = n_rot[...]
    for begin, end in ATTEND_GROUPS:
        stream.need(len(whole) + 2 * (end // step))
        fresh = []
        for t in range(begin, end):
            used = jnp.where(t < counts[0], lengths[t], 0)
            q = q_lat[t]
            rot = q_rot[t].T
            part = (mul(q, c_lat[t], 1, 1) + mul(rot, c_rot[t])) * scale
            scores[t] = jnp.where(position < used, part, -jnp.inf)
            both = (mul(q, fresh_lat, 1, 1) + mul(rot, fresh_rot, 1, 1)) * scale
            fresh.append(both[:, t : t + 1])
        for t in range(begin, end):
            part = scores[t]
            new = fresh[t - begin]
            top = jnp.maximum(jnp.max(part, axis=1, keepdims=True), new)
            expo = jnp.exp(part - top)
            fresh_expo = jnp.exp(new - top)
            inverse = 1.0 / (jnp.sum(expo, axis=1, keepdims=True) + fresh_expo)
            probs = (expo * inverse).astype(BF16)
            fresh_prob = (fresh_expo * inverse).astype(BF16).astype(F32)
            o = mul(probs, c_lat[t]) + fresh_prob * fresh_lat[t : t + 1].astype(F32)
            for j in range(width // 128):
                acc[j, pl.ds(t, heads, stride=rows), :] = o[:, j * 128 : (j + 1) * 128]
    leaving = []
    for j in range(width // 128):
        out[:, j * 128 : (j + 1) * 128] = acc[j].astype(BF16)
        leaving.append(send_out(out, out_hbm, j, 128, sems, len(copies)))
    for c in leaving:
        c.wait()


def attend(scale, q_latent, q_rope, cache_latent, cache_rope, new_latent, new_rope, lengths, counts):
    rows, heads, width = q_latent.shape
    positions = cache_latent.shape[1]

    def body(*refs):
        attend_kernel(scale, *refs)

    size = 2 * (q_latent.size * 2 + cache_latent.size + q_rope.size + cache_rope.size)
    flops = 4 * rows * heads * positions * width
    return pl.pallas_call(
        body,
        out_shape=jax.ShapeDtypeStruct((heads * rows, width), BF16),
        in_specs=[HBM] * 8,
        out_specs=HBM,
        scratch_shapes=[
            pltpu.SMEM(lengths.shape, jnp.int32),
            pltpu.SMEM(counts.shape, jnp.int32),
            pltpu.VMEM(new_latent.shape, BF16),
            pltpu.VMEM(new_rope.shape, BF16),
            pltpu.VMEM(q_latent.shape, BF16),
            pltpu.VMEM(q_rope.shape, BF16),
            pltpu.VMEM(cache_latent.shape, BF16),
            pltpu.VMEM(cache_rope.shape, BF16),
            pltpu.VMEM((rows, heads, positions), F32),
            pltpu.VMEM((width // 128, heads * rows, 128), F32),
            pltpu.VMEM((heads * rows, width), BF16),
            pltpu.SemaphoreType.DMA((6 + rows + width // 128,)),
        ],
        compiler_params=pltpu.CompilerParams(vmem_limit_bytes=VMEM_BYTES),
        cost_estimate=cost(flops, size),
        name="attend",
    )(lengths, counts, new_latent, new_rope, q_latent, q_rope, cache_latent, cache_rope)


def project_kernel(
    block, core_ref, got_hbm, uv1_hbm, uv2_hbm, wo1_hbm, wo2_hbm, out_hbm, got, uv, wo, heads_v, out, sems
):
    chips, span, width = got.shape
    heads, _, hv = uv1_hbm.shape
    rows = span // (2 * heads)
    depth, cols = wo1_hbm.shape
    copies = [pltpu.make_async_copy(got_hbm, got, sems.at[0])]
    for i, src in enumerate((uv1_hbm, uv2_hbm)):
        to = uv.at[pl.ds(i * heads, heads)]
        copies.append(pltpu.make_async_copy(src, to, sems.at[len(copies)]))
    for n in range(cols // block):
        at = pl.ds(n * block, block)
        for i, src in enumerate((wo1_hbm, wo2_hbm)):
            to = wo.at[pl.ds(i * depth, depth), at]
            copies.append(pltpu.make_async_copy(src.at[:, at], to, sems.at[len(copies)]))
    stream = Stream(copies, IN_FLIGHT + 3)
    stream.need(1)
    core = core_ref[0]
    half = heads * rows
    for s in range(2):
        which = core if s == 0 else 1 - core
        mine = got[:, pl.ds(pl.multiple_of(which * half, half), half), :].astype(F32)
        stream.need(s + 2)
        for i in range(heads):
            x = mine[:, i * rows : (i + 1) * rows, :].reshape(chips * rows, width).astype(BF16)
            n = s * heads + i
            heads_v[:, n * hv : (n + 1) * hv] = mul(x, uv[n]).astype(BF16)
    x = heads_v[...]
    leaving = []
    for n in range(cols // block):
        stream.need(3 + 2 * (n + 1))
        at = slice(n * block, (n + 1) * block)
        out[:, at] = mul(x, wo[:, at]).astype(BF16)
        leaving.append(send_out(out, out_hbm, n, block, sems, len(copies)))
    for c in leaving:
        c.wait()


def project(core, got, w_uv, w_uv2, w_o, w_o2):
    chips, span, width = got.shape
    heads, _, hv = w_uv.shape
    rows = chips * span // (2 * heads)
    depth, cols = w_o.shape
    block = 896

    def body(*refs):
        project_kernel(block, *refs)

    size = 2 * (got.size + 2 * w_uv.size + 2 * w_o.size + rows * cols)
    return pl.pallas_call(
        body,
        out_shape=jax.ShapeDtypeStruct((rows, cols), BF16),
        in_specs=[SMEM, HBM, HBM, HBM, HBM, HBM],
        out_specs=HBM,
        scratch_shapes=[
            pltpu.VMEM(got.shape, BF16),
            pltpu.VMEM((2 * heads, width, hv), BF16),
            pltpu.VMEM((2 * depth, cols), BF16),
            pltpu.VMEM((rows, 2 * depth), BF16),
            pltpu.VMEM((rows, cols), BF16),
            pltpu.SemaphoreType.DMA((3 + 3 * (cols // block),)),
        ],
        compiler_params=pltpu.CompilerParams(vmem_limit_bytes=PROJECT_BYTES),
        cost_estimate=cost(4 * rows * w_o.size, size),
        name="project",
    )(core, got, w_uv, w_uv2, w_o, w_o2)


def spans(first, size, total):
    edges = [0] + list(range(first, total, size)) + [total]
    return list(zip(edges[:-1], edges[1:]))


def feed_kernel(
    pieces, piece, block, x_ref, gate1, up1, gate2, up2, down1, down2, out_ref, gate_w, up_w, down_w, act, sems
):
    hidden, width = gate1.shape
    count = 0

    def copy(src, dst, rows, to, cols):
        nonlocal count
        count += 1
        return pltpu.make_async_copy(
            src.at[rows, cols], dst.at[to, cols], sems.at[count - 1]
        )

    everything = pl.ds(0, width)
    copies, ready = [], []
    for lo, hi in pieces:
        for dst, pair in ((gate_w, (gate1, gate2)), (up_w, (up1, up2))):
            for core, src in enumerate(pair):
                a, b = max(lo, core * hidden), min(hi, (core + 1) * hidden)
                for c in range(a, b, piece):
                    size = min(piece, b - c)
                    rows = pl.ds(c - core * hidden, size)
                    copies.append(copy(src, dst, rows, pl.ds(c, size), everything))
        ready.append(len(copies))
    for n in range(width // block):
        cols = pl.ds(n * block, block)
        for core, src in enumerate((down1, down2)):
            rows, to = pl.ds(0, hidden), pl.ds(core * hidden, hidden)
            copies.append(copy(src, down_w, rows, to, cols))
    stream = Stream(copies, IN_FLIGHT)
    x = x_ref[...]
    for (lo, hi), count in zip(pieces, ready):
        stream.need(count)
        gate = mul(x, gate_w[lo:hi], 1, 1)
        upper = mul(x, up_w[lo:hi], 1, 1)
        act[:, lo:hi] = (gate / (1.0 + jnp.exp(-gate)) * upper).astype(BF16)
    activated = act[...]
    for n in range(width // block):
        stream.need(ready[-1] + 2 * (n + 1))
        at = slice(n * block, (n + 1) * block)
        out_ref[:, at] = mul(activated, down_w[:, at]).astype(BF16)


def feed(x, *weights):
    rows, width = x.shape
    hidden = weights[0].shape[0]
    block = width // 2
    pieces = spans(128, 256, 2 * hidden)

    def body(*refs):
        feed_kernel(pieces, 96, block, *refs)

    size = 2 * (2 * x.size + sum(w.size for w in weights))
    return pl.pallas_call(
        body,
        out_shape=jax.ShapeDtypeStruct((rows, width), BF16),
        in_specs=[VMEM] + [HBM] * 6,
        out_specs=VMEM,
        scratch_shapes=[pltpu.VMEM((2 * hidden, width), BF16)] * 3
        + [
            pltpu.VMEM((rows, 2 * hidden), BF16),
            pltpu.SemaphoreType.DMA((48,)),
        ],
        compiler_params=pltpu.CompilerParams(vmem_limit_bytes=ROOMY_BYTES),
        cost_estimate=cost(12 * rows * weights[0].size, size),
        name="feed",
    )(x, *weights)


def solution(mesh):
    n_dp = mesh.shape["dp"]
    chips = n_dp // 2
    swap = [(i, i ^ 1) for i in range(n_dp)]
    same_core = [[2 * c + k for c in range(chips)] for k in range(2)]

    def sibling(w):
        return lax.ppermute(w, "dp", swap)

    def exchange(v):
        return lax.all_to_all(v, "dp", 0, 0, axis_index_groups=same_core, tiled=True)

    def summed(part, rows):
        got = exchange(part).reshape(chips, rows, part.shape[-1])
        return jnp.sum(got.astype(F32), axis=0)

    def on_device(
        residual_in,
        q_latent,
        q_rope,
        cache_latent,
        cache_rope,
        new_latent,
        new_rope,
        lengths,
        counts,
        w_uv,
        w_o,
        norm_gain,
        w_gate,
        w_up,
        w_down,
    ):
        rows = residual_in.shape[0]
        core = (lax.axis_index("dp") & 1).astype(jnp.int32).reshape(1)
        gate_t, up_t = w_gate.T, w_up.T
        w_uv2, w_o2 = sibling(w_uv), sibling(w_o)
        gate2, up2, down2 = sibling(gate_t), sibling(up_t), sibling(w_down)
        scale = (w_uv.shape[2] + q_rope.shape[1]) ** (-0.5)
        o_latent = attend(
            scale, q_latent, q_rope, cache_latent, cache_rope, new_latent, new_rope, lengths, counts
        )
        got = exchange(o_latent).reshape(chips, -1, o_latent.shape[1])
        got, gate2, up2, down2 = lax.optimization_barrier((got, gate2, up2, down2))
        part = project(core, got, w_uv, w_uv2, w_o, w_o2)
        hidden_mine = residual_in.astype(F32) + summed(part, rows)
        normed_mine = normalize(hidden_mine, norm_gain)
        copies = jnp.broadcast_to(normed_mine[None], (chips,) + normed_mine.shape)
        normed = exchange(copies.reshape(chips * rows, -1))
        part = feed(normed, gate_t, up_t, gate2, up2, w_down, down2)
        return (hidden_mine + summed(part, rows)).astype(BF16)

    placed = (
        P(("rep", "dp"), None),
        P(("rep", "dp"), None, None),
        P(("rep", "dp"), None, None),
        P(("rep", "dp"), None, None),
        P(("rep", "dp"), None, None),
        P(("rep", "dp"), None),
        P(("rep", "dp"), None),
        P(("rep", "dp")),
        P(("rep", "dp")),
        P("dp", None, None),
        P("dp", None),
        P(),
        P(None, "dp"),
        P(None, "dp"),
        P("dp", None),
    )
    return jax.shard_map(
        on_device, mesh=mesh, in_specs=placed, out_specs=P(("rep", "dp"), None), check_vma=False
    )
```
